32 devices in a mesh: grp: 4 (over y, x), blk: 8 (over z, core).
Axes of the slice: x: 2, y: 2, z: 4, core: 2. Of those that a mesh axis runs over, the one named last changes fastest.
Arguments:
- source_emb: bfloat16 [6144, 768], P('blk'), may hold values from -32 to 32
- target_emb: bfloat16 [6144, 768], P(('grp', 'blk')), may hold values from -16 to 16
- hard_pool: bfloat16 [6144, 768], P(('grp', 'blk')), may hold values from -16 to 16
- hard_index: int32 [6144], P('blk'), may hold values from 0 to 6143, as said below
- language: int32 [6144], P('blk'), may hold values from 0 to 108
- margin: float32 [109], replicated, may hold values from 0.5 to 3
Outputs:
- row_loss: float32 [6144], P('blk')
- source_grad: float32 [6144, 768], P('blk')
- target_grad: float32 [6144, 768], P(('grp', 'blk'))
- pool_grad: float32 [6144, 768], P(('grp', 'blk'))
The draws below stay inside these ranges and needn't reach their ends.
Inputs may be any that keep to these rules, and one draw needn't show every extreme that they name: `hard_index`: each entry is a row of hard_pool; an entry's owner is its value // 192. Within each aligned block of 192 entries no owner is named more than 12 times, and one owner, the same for all blocks, is named exactly 12 times in every block.
All inputs are finite; a program needn't handle non-finite values.
Results may differ from the reference program's by a relative error of at most 0.0025.
Values may be sent and summed in bfloat16 or wider, within the bound.
A program may use at most 64 MiB of HBM per device.

```python
import math
import jax
import jax.numpy as jnp
import numpy as np
from jax import lax

D = 768
LANGS = 109
TGT_DEV = 192
OWNERS = 32
HN_CAP = 12
SRC_DEV = 768
N = 6144


def clipped_normal(key, shape):
    return jnp.clip(jax.random.normal(key, shape, jnp.float32), -6.0, 6.0)


def entries(key, shape):
    return clipped_normal(key, shape)


def spread(key, low, high):
    return jnp.exp(jax.random.uniform(key, (N, 1), jnp.float32, math.log(low), math.log(high)))


def target_values(key):
    base = entries(jax.random.fold_in(key, 11), (N, D))
    scale_t = spread(jax.random.fold_in(key, 13), 0.5, 2.0)
    values = base * scale_t
    return values


def pool_values(key):
    base = entries(jax.random.fold_in(key, 31), (N, D))
    return base * spread(jax.random.fold_in(key, 33), 0.5, 2.0)


def hard_ids(key):
    special = jax.random.randint(jax.random.fold_in(key, 52), (), 1, OWNERS - 1, jnp.int32)
    slot_total = OWNERS * HN_CAP
    slot_ids = jnp.arange(slot_total, dtype=jnp.int32)
    slot_owner = slot_ids // HN_CAP

    def one_block(block_key, block_at):
        order_key, place_key, row_key = jax.random.split(block_key, 3)
        priority = jax.random.permutation(order_key, slot_total).astype(jnp.int32)
        priority = jnp.where(slot_owner == special, priority + slot_total, priority)
        first = block_at == 0
        priority = jnp.where(first & (slot_ids == 0), -2, priority)
        priority = jnp.where(first & (slot_ids == (OWNERS - 1) * HN_CAP), -1, priority)
        taken = jnp.argsort(priority, stable=True)[:TGT_DEV - HN_CAP]
        owners = jnp.concatenate([jnp.full((HN_CAP,), special, jnp.int32), slot_owner[taken]])
        places = jax.random.permutation(place_key, TGT_DEV).astype(jnp.int32)
        owner_of = owners[places]
        row_of = jax.random.randint(row_key, (TGT_DEV,), 0, TGT_DEV, jnp.int32)
        row_of = jnp.where(first & (owner_of == 0), 0, jnp.where(first & (owner_of == OWNERS - 1), TGT_DEV - 1, row_of))
        return (owner_of * TGT_DEV + row_of).astype(jnp.int32)
    block_keys = jax.random.split(jax.random.fold_in(key, 51), OWNERS)
    return jax.vmap(one_block)(block_keys, jnp.arange(OWNERS, dtype=jnp.int32)).reshape(N)


def draw_target_emb(key, part):
    return target_values(key).astype(jnp.bfloat16)


def draw_hard_pool(key, part):
    return pool_values(key).astype(jnp.bfloat16)


def draw_hard_index(key, part):
    return hard_ids(key)


def draw_source_emb(key, part):
    targets = target_values(key)
    pooled = pool_values(key)
    chosen = hard_ids(key)
    noise = entries(jax.random.fold_in(key, 41), (N, D))
    row_scale = spread(jax.random.fold_in(key, 42), 0.3, 3.0)
    values = row_scale * (6.0 / D) * (targets + pooled[chosen] + noise)
    return values.astype(jnp.bfloat16)


def with_ends(drawn, own_key, low, top_value):
    place = [jax.random.randint(jax.random.fold_in(own_key, axis), (), 0, length) for axis, length in enumerate(drawn.shape)]
    longest = drawn.shape.index(max(drawn.shape))
    neighbour = place[:longest] + [(place[longest] + 1) % drawn.shape[longest]] + place[longest + 1:]
    return drawn.at[tuple(place)].set(low).at[tuple(neighbour)].set(top_value)


def rank_bounds(number_of, skew):
    weights = [(1 << 20) // math.isqrt(grade ** skew) + 1 for grade in range(1, number_of + 1)]
    scale = 1 + sum(weights) // (1 << 30)
    return np.cumsum(np.array([max(1, weight // scale) for weight in weights]))


def skewed_ids(stream_key, dims, number_of, skew):
    grid = rank_bounds(number_of, skew)
    ticket = jax.random.randint(jax.random.fold_in(stream_key, 1), dims, 0, int(grid[number_of - 1]))
    grade = jnp.searchsorted(jnp.asarray(grid, jnp.int32), ticket, side="right")
    return jax.random.permutation(jax.random.fold_in(stream_key, 2), number_of)[grade].astype(jnp.int32)


def setup_inputs(seed: int = 0) -> dict:
    seeds = jax.random.split(jax.random.key(seed), 7)
    return {
        "source_emb": draw_source_emb(jax.random.fold_in(seeds[6], 71), 0),
        "target_emb": draw_target_emb(jax.random.fold_in(seeds[6], 71), 0),
        "hard_pool": draw_hard_pool(jax.random.fold_in(seeds[6], 71), 0),
        "hard_index": draw_hard_index(jax.random.fold_in(seeds[6], 71), 0),
        "language": with_ends(skewed_ids(seeds[4], (N,), LANGS, 2), jax.random.fold_in(seeds[4], 3), 0, LANGS - 1).astype(jnp.int32),
        "margin": jnp.clip(jax.random.uniform(seeds[5], (LANGS,), jnp.float32, 0.5, 3.0), 0.5, 3.0),
    }


def reference(source_emb, target_emb, hard_pool, hard_index, language, margin):
    total_rows = source_emb.shape[0]
    width = source_emb.shape[1]
    margin_row = margin[language]
    hard_rows = hard_pool[hard_index]
    hard_score = jnp.sum(source_emb.astype(jnp.float32) * hard_rows.astype(jnp.float32), axis=1)
    block_rows = SRC_DEV
    block_count = total_rows // block_rows
    columns = jnp.arange(total_rows, dtype=jnp.int32)

    def one_block(grad_sum, block_at):
        start = (block_at * block_rows).astype(jnp.int32)
        sources = lax.dynamic_slice_in_dim(source_emb, start, block_rows, 0)
        margins = lax.dynamic_slice_in_dim(margin_row, start, block_rows, 0)
        hard_part = lax.dynamic_slice_in_dim(hard_score, start, block_rows, 0)
        hard_block = lax.dynamic_slice_in_dim(hard_rows, start, block_rows, 0)
        row_ids = start + jnp.arange(block_rows, dtype=jnp.int32)
        scores = jnp.dot(sources, target_emb.T, preferred_element_type=jnp.float32)
        positive = row_ids[:, None] == columns[None, :]
        adjusted = scores - jnp.where(positive, margins[:, None], jnp.float32(0.0))
        row_top = jnp.maximum(jnp.max(adjusted, axis=1), hard_part)
        row_total = jnp.sum(jnp.exp(adjusted - row_top[:, None]), axis=1) + jnp.exp(hard_part - row_top)
        log_total = row_top + jnp.log(row_total)
        row_loss = log_total - jnp.sum(jnp.where(positive, adjusted, jnp.float32(0.0)), axis=1)
        prob_tile = (jnp.exp(adjusted - log_total[:, None]) - positive.astype(jnp.float32)).astype(jnp.bfloat16)
        hard_prob = jnp.exp(hard_part - log_total)
        source_grad = jnp.dot(prob_tile, target_emb, preferred_element_type=jnp.float32)
        source_grad = source_grad + hard_prob[:, None] * hard_block.astype(jnp.float32)
        grad_sum = grad_sum + jnp.dot(prob_tile.T, sources, preferred_element_type=jnp.float32)
        return grad_sum, (row_loss, source_grad, hard_prob)

    start_grad = jnp.zeros((total_rows, width), jnp.float32)
    grad_sum, outputs = lax.scan(one_block, start_grad, jnp.arange(block_count, dtype=jnp.int32))
    row_loss = outputs[0].reshape(total_rows)
    source_grad = outputs[1].reshape(total_rows, width)
    hard_prob = outputs[2].reshape(total_rows)
    contribution = hard_prob[:, None] * source_emb.astype(jnp.float32)
    pool_grad = jnp.zeros((total_rows, width), jnp.float32).at[hard_index].add(contribution)
    return (row_loss, source_grad, grad_sum, pool_grad)
```

```python
import functools

import jax
import jax.numpy as jnp
from jax import lax
from jax.experimental import pallas as pl
from jax.experimental.pallas import tpu as pltpu
from jax.sharding import PartitionSpec as P

neg_fill = -1e30
f32 = jnp.float32
bf16 = jnp.bfloat16
MESH = pl.DeviceIdType.MESH


def dot_nt(a, b):
    return lax.dot_general(a, b, (((1,), (1,)), ((), ())), preferred_element_type=f32)


def dot_tn(a, b):
    return lax.dot_general(a, b, (((0,), (0,)), ((), ())), preferred_element_type=f32)


def dot_nn(a, b):
    return lax.dot_general(a, b, (((1,), (0,)), ((), ())), preferred_element_type=f32)


def kernel(
    dims,
    src, tgt, pool, rows_in, margin_col,
    loss_out, sgrad, tgrad, pgrad,
    tall, adj, prob, sel, want_send, want_recv, picks, slots_send, slots_recv, hp_send, hp_recv,
    stats, sg_send, sg_recv, sib_send, sib_recv, rs_send, rs_recv,
    t_ss, t_rs, fw_ss, w_ss, w_rs, p_ss, p_rs, s_ss, s_rs, h_ss, h_rs, st_ss, st_rs,
    q_ss, q_rs, a_ss, a_rs, b_ss, b_rs, r_ss, r_rs,
):
    B, G, M, T, D, cap = dims
    Z = B // 2
    N1 = B * T
    W = 256
    b = lax.axis_index("blk")
    g = lax.axis_index("grp")
    z = b // 2
    c = b % 2
    sib = z * 2 + (1 - c)

    def blk_of(dz, core):
        return ((z + dz) % Z) * 2 + core

    def trows(j):
        return pl.ds(pl.multiple_of(j * T, T), T)

    def frows(j):
        return pl.ds(pl.multiple_of(N1 + j * cap, 16), cap)

    def crows(j):
        return pl.ds(pl.multiple_of(j * cap, 16), cap)

    def to_blk(src_ref, dst_ref, ss, rs, peer):
        return pltpu.make_async_remote_copy(
            src_ref=src_ref, dst_ref=dst_ref, send_sem=ss, recv_sem=rs,
            device_id={"blk": peer}, device_id_type=MESH,
        )

    def to_grp(src_ref, dst_ref, ss, rs, peer):
        return pltpu.make_async_remote_copy(
            src_ref=src_ref, dst_ref=dst_ref, send_sem=ss, recv_sem=rs,
            device_id={"grp": peer}, device_id_type=MESH,
        )

    barrier = pltpu.get_barrier_semaphore()
    for k in range(1, B):
        pl.semaphore_signal(barrier, inc=1, device_id={"blk": (b + k) % B}, device_id_type=MESH)
    for k in range(1, G):
        pl.semaphore_signal(barrier, inc=1, device_id={"grp": (g + k) % G}, device_id_type=MESH)

    owner_row = rows_in[0:1, :]
    loc_row = rows_in[1:2, :]
    present = owner_row >= 0
    col_id = lax.broadcasted_iota(jnp.int32, (T, M), 1)
    row_id = lax.broadcasted_iota(jnp.int32, (T, M), 0)

    R = max(B, 16)
    named = owner_row == lax.broadcasted_iota(jnp.int32, (R, M), 0)
    named_hot = jnp.where(named, 1.0, 0.0).astype(bf16)
    before = jnp.zeros((R, M), f32)
    for n in range(M // W):
        earlier = lax.broadcasted_iota(jnp.int32, (W, M), 0) + n * W < lax.broadcasted_iota(
            jnp.int32, (W, M), 1
        )
        step = jnp.where(earlier, 1.0, 0.0).astype(bf16)
        before = before + dot_nn(named_hot[:, n * W : (n + 1) * W], step)
    rank = jnp.sum(jnp.where(named, before, 0.0), axis=0, keepdims=True).astype(jnp.int32)
    slot = jnp.where(present, owner_row * cap + rank, -1)

    slot_id = lax.broadcasted_iota(jnp.int32, (cap, M), 0)
    loc8 = jnp.broadcast_to((loc_row + 1).astype(f32).astype(bf16), (8, M))

    def fill_sel(j, carry):
        hot = jnp.where(slot == slot_id + j * cap, 1.0, 0.0).astype(bf16)
        sel[crows(j), :] = hot
        want_send[j, :, 0:cap] = dot_nt(loc8, hot) - 1.0
        return carry

    lax.fori_loop(0, B, fill_sel, 0)

    pl.semaphore_wait(barrier, B - 1 + G - 1)

    sends = []
    for k in range(1, B):
        peer = (b + k) % B
        cp = to_blk(want_send.at[peer], want_recv.at[b], w_ss.at[k], w_rs.at[b], peer)
        cp.start()
        sends.append(cp)
    cp = to_blk(tgt, tall.at[trows(b)], t_ss.at[0], t_rs.at[b], sib)
    cp.start()
    sends.append(cp)
    for dz in range(1, Z):
        cp = to_blk(tgt, tall.at[trows(b)], t_ss.at[dz], t_rs.at[b], blk_of(dz, c))
        cp.start()
        sends.append(cp)
    tall[trows(b), :] = tgt[...]
    want_recv[b] = want_send[b]

    lang_id = lax.broadcasted_iota(jnp.int32, (margin_col.shape[0], M), 0)
    margin_row = jnp.sum(
        jnp.where(rows_in[2:3, :] == lang_id, margin_col[...], 0.0), axis=0, keepdims=True
    )

    def hit(j):
        return row_id - col_id == b * M - (g * B + j) * T

    def score(j, carry):
        top, pos = carry
        s = dot_nt(tall[trows(j), :], src[...])
        diag = hit(j)
        s = s - jnp.where(diag, margin_row, 0.0)
        adj[trows(j), :] = s
        top = jnp.maximum(top, jnp.max(s, axis=0, keepdims=True))
        pos = pos + jnp.sum(jnp.where(diag, s, 0.0), axis=0, keepdims=True)
        return top, pos

    carry = (jnp.full((1, M), neg_fill, f32), jnp.zeros((1, M), f32))
    carry = score(b, carry)

    pool_id = lax.broadcasted_iota(jnp.int32, (T, cap), 0).astype(f32)
    for k in range(0, B):
        peer = (b + k) % B
        if k:
            to_blk(want_send.at[0], want_recv.at[peer], w_ss.at[0], w_rs.at[peer], peer).wait_recv()
        hot = jnp.where(pool_id == want_recv[peer, 0:1, 0:cap], 1.0, 0.0).astype(bf16)
        picked = dot_tn(hot, pool[...]).astype(bf16)
        if k == 0:
            tall[frows(b), :] = picked
        else:
            picks[k - 1] = picked
            cp = to_blk(picks.at[k - 1], tall.at[frows(b)], p_ss.at[k], p_rs.at[b], peer)
            cp.start()
            sends.append(cp)

    def wait_t(j):
        to_blk(tgt, tall.at[trows(j)], t_ss.at[0], t_rs.at[j], sib).wait_recv()

    wait_t(sib)
    carry = score(sib, carry)
    for dz in range(1, Z):
        near = blk_of(dz, c)
        wait_t(near)
        cp = to_blk(tall.at[trows(near)], tall.at[trows(near)], fw_ss.at[dz], t_rs.at[near], sib)
        cp.start()
        sends.append(cp)
        carry = score(near, carry)
    def fill_slots(j, carry):
        slots_send[j] = dot_nn(sel[crows(j), :], src[...]).astype(bf16)
        return carry

    lax.fori_loop(0, B, fill_slots, 0)
    for k in range(1, B):
        peer = (b + k) % B
        cp = to_blk(slots_send.at[peer], slots_recv.at[b], s_ss.at[k], s_rs.at[b], peer)
        cp.start()
        sends.append(cp)
    slots_recv[b] = slots_send[b]
    for dz in range(1, Z):
        far = blk_of(dz, 1 - c)
        wait_t(far)
        carry = score(far, carry)
    top, pos = carry
    for k in range(1, B):
        peer = (b + k) % B
        to_blk(picks.at[0], tall.at[frows(peer)], p_ss.at[0], p_rs.at[peer], peer).wait_recv()

    def hard_part(j, acc):
        s = dot_nt(tall[frows(j), :], src[...])
        return acc + jnp.sum(s * sel[crows(j), :].astype(f32), axis=0, keepdims=True)

    hard = lax.fori_loop(0, B, hard_part, jnp.zeros((1, M), f32))
    hard = jnp.where(present, hard, neg_fill)
    top = jnp.maximum(top, hard)

    def add_exp(j, acc):
        return acc + jnp.sum(jnp.exp(adj[trows(j), :] - top), axis=0, keepdims=True)

    total = jnp.where(present, jnp.exp(hard - top), 0.0)
    total = lax.fori_loop(0, B, add_exp, total)
    stats[g, 0:1, :] = top
    stats[g, 1:2, :] = total
    stats[g, 2:3, :] = pos
    for k in range(1, G):
        peer = (g + k) % G
        cp = to_grp(stats.at[g], stats.at[g], st_ss.at[k], st_rs.at[g], peer)
        cp.start()
        sends.append(cp)
    for k in range(1, G):
        peer = (g + k) % G
        to_grp(stats.at[g], stats.at[peer], st_ss.at[0], st_rs.at[peer], peer).wait_recv()
    all_top = stats[0, 0:1, :]
    for q in range(1, G):
        all_top = jnp.maximum(all_top, stats[q, 0:1, :])
    all_total = jnp.zeros((1, M), f32)
    all_pos = jnp.zeros((1, M), f32)
    for q in range(G):
        all_total = all_total + stats[q, 1:2, :] * jnp.exp(stats[q, 0:1, :] - all_top)
        all_pos = all_pos + stats[q, 2:3, :]
    log_total = all_top + jnp.log(all_total)
    loss_out[...] = log_total - all_pos
    hard_prob = jnp.where(present, jnp.exp(hard - log_total), 0.0)

    hp_hi = hard_prob.astype(bf16)
    rest = hard_prob - hp_hi.astype(f32)
    hp_mid = rest.astype(bf16)
    hp_lo = (rest - hp_mid.astype(f32)).astype(bf16)
    part_id = lax.broadcasted_iota(jnp.int32, (8, M), 0)
    hp8 = jnp.where(
        part_id == 0,
        hp_hi.astype(f32),
        jnp.where(
            part_id == 1, hp_mid.astype(f32), jnp.where(part_id == 2, hp_lo.astype(f32), 0.0)
        ),
    ).astype(bf16)

    def fill_hp(j, carry):
        hp_send[j, :, 0:cap] = dot_nt(hp8, sel[crows(j), :])
        return carry

    lax.fori_loop(0, B, fill_hp, 0)
    for k in range(1, B):
        peer = (b + k) % B
        cp = to_blk(hp_send.at[peer], hp_recv.at[b], h_ss.at[k], h_rs.at[b], peer)
        cp.start()
        sends.append(cp)
    hp_recv[b] = hp_send[b]

    def make_prob(j, carry):
        p = jnp.exp(adj[trows(j), :] - log_total) - jnp.where(hit(j), 1.0, 0.0)
        prob[trows(j), :] = p.astype(bf16)
        return carry

    lax.fori_loop(0, B, make_prob, 0)

    def fill_hard(j, carry):
        hot = sel[crows(j), :].astype(f32)
        prob[frows(j), :] = (hot * hp_hi.astype(f32)).astype(bf16)
        sel[crows(j), :] = (hot * hp_mid.astype(f32)).astype(bf16)
        return carry

    lax.fori_loop(0, B, fill_hard, 0)

    for dz in range(Z):
        j = blk_of(dz, 1 - c)
        sib_send[dz] = dot_nn(prob[trows(j), :], src[...]).astype(bf16)
        cp = to_blk(sib_send.at[dz], sib_recv.at[dz], b_ss.at[dz], b_rs.at[dz], sib)
        cp.start()
        sends.append(cp)
    for dz in list(range(1, Z)) + [0]:
        j = blk_of(dz, c)
        term = dot_nn(prob[trows(j), :], src[...])
        to_blk(sib_send.at[0], sib_recv.at[dz], b_ss.at[0], b_rs.at[dz], sib).wait_recv()
        term = term + sib_recv[dz].astype(f32)
        if dz == 0:
            tgrad[...] = term
        else:
            rs_send[dz - 1] = term.astype(bf16)
            cp = to_blk(rs_send.at[dz - 1], rs_recv.at[dz - 1], r_ss.at[dz], r_rs.at[dz], j)
            cp.start()
            sends.append(cp)

    V = W if N1 <= 2048 else W // 2
    for n in range(M // V):
        cols = pl.ds(n * V, V)
        part = dot_tn(prob[:, cols], tall[...])
        part = part + dot_tn(sel[:, cols], tall[pl.ds(N1, B * cap), :])
        sgrad[pl.ds(n * V, V), :] = part
    for k in range(1, G):
        peer = (g + k) % G
        sg_send[k - 1] = sgrad[trows(peer), :].astype(bf16)
        cp = to_grp(sg_send.at[k - 1], sg_recv.at[k - 1], q_ss.at[k], q_rs.at[k], peer)
        cp.start()
        sends.append(cp)

    acc = jnp.zeros((T, D), f32)
    for k in range(0, B):
        peer = (b + k) % B
        if k:
            to_blk(slots_send.at[0], slots_recv.at[peer], s_ss.at[0], s_rs.at[peer], peer).wait_recv()
            to_blk(hp_send.at[0], hp_recv.at[peer], h_ss.at[0], h_rs.at[peer], peer).wait_recv()
        hot = pool_id == want_recv[peer, 0:1, 0:cap]
        weight = jnp.sum(hp_recv[peer, :, 0:cap], axis=0, keepdims=True)
        hi = weight.astype(bf16).astype(f32)
        rows = slots_recv[peer]
        acc = acc + dot_nn(jnp.where(hot, hi, 0.0).astype(bf16), rows)
        acc = acc + dot_nn(jnp.where(hot, weight - hi, 0.0).astype(bf16), rows)
    pgrad[...] = acc

    own = sgrad[trows(g), :]
    for k in range(1, G):
        to_grp(sg_send.at[0], sg_recv.at[k - 1], q_ss.at[0], q_rs.at[k], (g + k) % G).wait_recv()
        own = own + sg_recv[k - 1].astype(f32)
    sgrad[trows(g), :] = own
    for k in range(1, G):
        peer = (g + k) % G
        cp = to_grp(sgrad.at[trows(g)], sgrad.at[trows(g)], a_ss.at[k], a_rs.at[g], peer)
        cp.start()
        sends.append(cp)

    final = tgrad[...]
    for dz in range(1, Z):
        to_blk(rs_send.at[0], rs_recv.at[dz - 1], r_ss.at[0], r_rs.at[dz], sib).wait_recv()
        final = final + rs_recv[dz - 1].astype(f32)
    tgrad[...] = final
    for k in range(1, G):
        peer = (g + k) % G
        to_grp(sgrad.at[trows(g)], sgrad.at[trows(peer)], a_ss.at[0], a_rs.at[peer], peer).wait_recv()
    for cp in sends:
        cp.wait_send()


def shards(source_emb, target_emb, hard_pool, hard_index, language, margin):
    M, D = source_emb.shape
    T = target_emb.shape[0]
    B = lax.axis_size("blk")
    G = lax.axis_size("grp")
    owners = B * G
    per_block = max(2, (2 * T + owners - 1) // owners)
    cap = -(-(per_block * (M // T)) // 16) * 16
    Z = B // 2
    g = lax.axis_index("grp")
    owner = hard_index // T
    local = jnp.where(owner // B == g, owner % B, -1)
    rows_in = jnp.stack([local, hard_index % T, language])
    dims = (B, G, M, T, D, cap)
    dma = pltpu.SemaphoreType.DMA
    vmem = pl.BlockSpec(memory_space=pltpu.VMEM)
    K = B * T + B * cap
    flops = 2 * M * D * (3 * B * T + 4 * B * cap)
    loss, sg, tg, pg = pl.pallas_call(
        functools.partial(kernel, dims),
        out_shape=[
            jax.ShapeDtypeStruct((1, M), f32),
            jax.ShapeDtypeStruct((M, D), f32),
            jax.ShapeDtypeStruct((T, D), f32),
            jax.ShapeDtypeStruct((T, D), f32),
        ],
        in_specs=[vmem] * 5,
        out_specs=[vmem] * 4,
        scratch_shapes=[
            pltpu.VMEM((K, D), bf16),
            pltpu.VMEM((B * T, M), f32),
            pltpu.VMEM((K, M), bf16),
            pltpu.VMEM((B * cap, M), bf16),
            pltpu.VMEM((B, 8, 128), f32),
            pltpu.VMEM((B, 8, 128), f32),
            pltpu.VMEM((B - 1, cap, D), bf16),
            pltpu.VMEM((B, cap, D), bf16),
            pltpu.VMEM((B, cap, D), bf16),
            pltpu.VMEM((B, 8, 128), f32),
            pltpu.VMEM((B, 8, 128), f32),
            pltpu.VMEM((G, 8, M), f32),
            pltpu.VMEM((G - 1, T, D), bf16),
            pltpu.VMEM((G - 1, T, D), bf16),
            pltpu.VMEM((Z, T, D), bf16),
            pltpu.VMEM((Z, T, D), bf16),
            pltpu.VMEM((Z - 1, T, D), bf16),
            pltpu.VMEM((Z - 1, T, D), bf16),
            dma((Z,)), dma((B,)), dma((Z,)),
            dma((B,)), dma((B,)), dma((B,)), dma((B,)),
            dma((B,)), dma((B,)), dma((B,)), dma((B,)),
            dma((G,)), dma((G,)),
            dma((G,)), dma((G,)), dma((G,)), dma((G,)),
            dma((Z,)), dma((Z,)), dma((Z,)), dma((Z,)),
        ],
        compiler_params=pltpu.CompilerParams(
            collective_id=0, has_side_effects=True, vmem_limit_bytes=63 * 1024 * 1024
        ),
        cost_estimate=pl.CostEstimate(
            flops=flops, bytes_accessed=8 * M * D, transcendentals=2 * B * T * M
        ),
        name="loss_kernel",
    )(
        source_emb, target_emb, hard_pool, rows_in,
        margin.reshape(margin.shape[0], 1),
    )
    return loss.reshape(M), sg, tg, pg


def solution(mesh):
    in_specs = (
        P("blk", None),
        P(("grp", "blk"), None),
        P(("grp", "blk"), None),
        P("blk"),
        P("blk"),
        P(),
    )
    out_specs = (P("blk"), P("blk", None), P(("grp", "blk"), None), P(("grp", "blk"), None))
    return jax.shard_map(shards, mesh=mesh, in_specs=in_specs, out_specs=out_specs, check_vma=False)
```

```python
import functools

import jax
import jax.numpy as jnp
from jax import lax
from jax.experimental import pallas as pl
from jax.experimental.pallas import tpu as pltpu
from jax.sharding import PartitionSpec as P

neg_fill = -1e30
f32 = jnp.float32
bf16 = jnp.bfloat16
MESH = pl.DeviceIdType.MESH


def dot_nt(a, b):
    return lax.dot_general(a, b, (((1,), (1,)), ((), ())), preferred_element_type=f32)


def dot_tn(a, b):
    return lax.dot_general(a, b, (((0,), (0,)), ((), ())), preferred_element_type=f32)


def dot_nn(a, b):
    return lax.dot_general(a, b, (((1,), (0,)), ((), ())), preferred_element_type=f32)


def kernel(
    dims,
    src, tgt, pool, index_in, lang_in, margin_in,
    loss_out, sg_out, tgrad, pgrad,
    tall, adj, prob, sel, want_send, want_recv, picks, slots_send, slots_recv, hp_send, hp_recv,
    stats, line, mpad, sg_send, sg_recv, sib_send, sib_recv, rs_send, rs_recv,
    t_ss, t_rs, up_ss, dn_ss, fu_ss, fd_ss, w_ss, w_rs, p_ss, p_rs, s_ss, s_rs, h_ss, h_rs, st_ss, st_rs,
    q_ss, q_rs, a_ss, a_rs, b_ss, b_rs, r_ss, r_rs,
):
    B, G, M, T, D, cap = dims
    Z = B // 2
    N1 = B * T
    W = 256
    b = lax.axis_index("blk")
    g = lax.axis_index("grp")
    z = b // 2
    c = b % 2
    sib = z * 2 + (1 - c)

    def blk_of(dz, core):
        return ((z + dz) % Z) * 2 + core

    def trows(j):
        return pl.ds(pl.multiple_of(j * T, T), T)

    def frows(j):
        return pl.ds(pl.multiple_of(N1 + j * cap, 16), cap)

    def crows(j):
        return pl.ds(pl.multiple_of(j * cap, 16), cap)

    def to_blk(src_ref, dst_ref, ss, rs, peer):
        return pltpu.make_async_remote_copy(
            src_ref=src_ref, dst_ref=dst_ref, send_sem=ss, recv_sem=rs,
            device_id={"blk": peer}, device_id_type=MESH,
        )

    def to_grp(src_ref, dst_ref, ss, rs, peer):
        return pltpu.make_async_remote_copy(
            src_ref=src_ref, dst_ref=dst_ref, send_sem=ss, recv_sem=rs,
            device_id={"grp": peer}, device_id_type=MESH,
        )

    barrier = pltpu.get_barrier_semaphore()
    for k in range(1, B):
        pl.semaphore_signal(barrier, inc=1, device_id={"blk": (b + k) % B}, device_id_type=MESH)
    for k in range(1, G):
        pl.semaphore_signal(barrier, inc=1, device_id={"grp": (g + k) % G}, device_id_type=MESH)

    index_row = index_in[...]
    owner_row = jnp.full((1, M), -1, jnp.int32)
    loc_row = jnp.zeros((1, M), jnp.int32)
    for j in range(B):
        base = (g * B + j) * T
        inside = (index_row >= base) & (index_row < base + T)
        owner_row = jnp.where(inside, j, owner_row)
        loc_row = jnp.where(inside, index_row - base, loc_row)
    present = owner_row >= 0
    col_id = lax.broadcasted_iota(jnp.int32, (T, M), 1)
    row_id = lax.broadcasted_iota(jnp.int32, (T, M), 0)

    R = max(B, 16)
    named = owner_row == lax.broadcasted_iota(jnp.int32, (R, M), 0)
    named_hot = jnp.where(named, 1.0, 0.0).astype(bf16)
    before = jnp.zeros((R, M), f32)
    for n in range(M // W):
        earlier = lax.broadcasted_iota(jnp.int32, (W, M), 0) + n * W < lax.broadcasted_iota(
            jnp.int32, (W, M), 1
        )
        step = jnp.where(earlier, 1.0, 0.0).astype(bf16)
        before = before + dot_nn(named_hot[:, n * W : (n + 1) * W], step)
    rank = jnp.sum(jnp.where(named, before, 0.0), axis=0, keepdims=True).astype(jnp.int32)
    slot = jnp.where(present, owner_row * cap + rank, -1)

    slot_id = lax.broadcasted_iota(jnp.int32, (cap, M), 0)
    loc8 = jnp.broadcast_to((loc_row + 1).astype(f32).astype(bf16), (8, M))

    def fill_sel(j, carry):
        hot = jnp.where(slot == slot_id + j * cap, 1.0, 0.0).astype(bf16)
        sel[crows(j), :] = hot
        want_send[j, :, 0:cap] = dot_nt(loc8, hot) - 1.0
        return carry

    lax.fori_loop(0, B, fill_sel, 0)

    pl.semaphore_wait(barrier, B - 1 + G - 1)

    sends = []
    for k in range(1, B):
        peer = (b + k) % B
        cp = to_blk(want_send.at[peer], want_recv.at[b], w_ss.at[k], w_rs.at[b], peer)
        cp.start()
        sends.append(cp)
    cp = to_blk(tgt, tall.at[trows(b)], t_ss.at[0], t_rs.at[b], sib)
    cp.start()
    sends.append(cp)

    def up_copy(block, step):
        return to_blk(
            tall.at[trows(block)], tall.at[trows(block)], up_ss.at[step], t_rs.at[block], b + 2
        )

    def down_copy(block, step):
        return to_blk(
            tall.at[trows(block)], tall.at[trows(block)], dn_ss.at[step], t_rs.at[block], b - 2
        )

    def side_copy(block, sems, step):
        return to_blk(
            tall.at[trows(block)], tall.at[trows(block)], sems.at[step], t_rs.at[block], sib
        )

    has_up = z + 1 < Z
    has_down = z >= 1
    tall[trows(b), :] = tgt[...]

    @pl.when(has_up)
    def _():
        up_copy(b, 0).start()

    @pl.when(has_down)
    def _():
        down_copy(b, 0).start()

    want_recv[b] = want_send[b]

    mpad[...] = jnp.zeros_like(mpad)
    mpad[0:1, 0 : margin_in.shape[1]] = margin_in[...]
    m_all = mpad[0:1, :]
    m_hi = m_all.astype(bf16).astype(f32)
    m_mid = (m_all - m_hi).astype(bf16).astype(f32)
    m_lo = m_all - m_hi - m_mid
    m_id = lax.broadcasted_iota(jnp.int32, mpad.shape, 0)
    m_parts = jnp.where(
        m_id == 0, m_hi, jnp.where(m_id == 1, m_mid, jnp.where(m_id == 2, m_lo, 0.0))
    ).astype(bf16)
    lang_id = lax.broadcasted_iota(jnp.int32, (mpad.shape[1], M), 0)
    lang_hot = jnp.where(lang_in[...] == lang_id, 1.0, 0.0).astype(bf16)
    margin_row = jnp.sum(dot_nn(m_parts, lang_hot), axis=0, keepdims=True)

    def hit(j):
        return row_id - col_id == b * M - (g * B + j) * T

    line[0:1, :] = jnp.full((1, M), neg_fill, f32)
    line[1:2, :] = jnp.zeros((1, M), f32)
    line[2:3, :] = margin_row

    def score(j):
        s = dot_nt(tall[trows(j), :], src[...])
        diag = hit(j)
        s = s - jnp.where(diag, line[2:3, :], 0.0)
        adj[trows(j), :] = s
        line[0:1, :] = jnp.maximum(line[0:1, :], jnp.max(s, axis=0, keepdims=True))
        line[1:2, :] += jnp.sum(jnp.where(diag, s, 0.0), axis=0, keepdims=True)

    score(b)

    pool_id = lax.broadcasted_iota(jnp.int32, (T, cap), 0).astype(f32)
    for k in range(0, B):
        peer = (b + k) % B
        if k:
            to_blk(want_send.at[0], want_recv.at[peer], w_ss.at[0], w_rs.at[peer], peer).wait_recv()
        hot = jnp.where(pool_id == want_recv[peer, 0:1, 0:cap], 1.0, 0.0).astype(bf16)
        picked = dot_tn(hot, pool[...]).astype(bf16)
        if k == 0:
            tall[frows(b), :] = picked
        else:
            picks[k - 1] = picked
            cp = to_blk(picks.at[k - 1], tall.at[frows(b)], p_ss.at[k], p_rs.at[b], peer)
            cp.start()
            sends.append(cp)

    def wait_t(j):
        to_blk(tgt, tall.at[trows(j)], t_ss.at[0], t_rs.at[j], sib).wait_recv()

    wait_t(sib)
    score(sib)

    def pass_on(step, carry):
        below = z - 1 - step
        above = z + 1 + step

        @pl.when(below >= 0)
        def _():
            block = below * 2 + c
            wait_t(block)

            @pl.when(has_up)
            def _():
                up_copy(block, step + 1).start()

            side_copy(block, fu_ss, step).start()

        @pl.when(above < Z)
        def _():
            block = above * 2 + c
            wait_t(block)

            @pl.when(has_down)
            def _():
                down_copy(block, step + 1).start()

            side_copy(block, fd_ss, step).start()

        def use(q, inner):
            at = jnp.where(q % 2 == 0, below, above)

            @pl.when((at >= 0) & (at < Z))
            def _():
                far = q // 2
                block = at * 2 + (c + far) % 2

                @pl.when(far == 1)
                def _():
                    wait_t(block)

                score(block)

            return inner

        lax.fori_loop(0, 4, use, 0)
        return carry

    def fill_slots(j, carry):
        slots_send[j] = dot_nn(sel[crows(j), :], src[...]).astype(bf16)
        return carry

    lax.fori_loop(0, B, fill_slots, 0)
    lax.fori_loop(0, Z - 1, pass_on, 0)
    for k in range(1, B):
        peer = (b + k) % B
        cp = to_blk(slots_send.at[peer], slots_recv.at[b], s_ss.at[k], s_rs.at[b], peer)
        cp.start()
        sends.append(cp)
    slots_recv[b] = slots_send[b]
    top = line[0:1, :]
    pos = line[1:2, :]
    for k in range(1, B):
        peer = (b + k) % B
        to_blk(picks.at[0], tall.at[frows(peer)], p_ss.at[0], p_rs.at[peer], peer).wait_recv()

    def hard_part(j, acc):
        s = dot_nt(tall[frows(j), :], src[...])
        return acc + jnp.sum(s * sel[crows(j), :].astype(f32), axis=0, keepdims=True)

    hard = lax.fori_loop(0, B, hard_part, jnp.zeros((1, M), f32))
    hard = jnp.where(present, hard, neg_fill)
    top = jnp.maximum(top, hard)

    def add_exp(j, acc):
        return acc + jnp.sum(jnp.exp(adj[trows(j), :] - top), axis=0, keepdims=True)

    total = jnp.where(present, jnp.exp(hard - top), 0.0)
    total = lax.fori_loop(0, B, add_exp, total)
    stats[g, 0:1, :] = top
    stats[g, 1:2, :] = total
    stats[g, 2:3, :] = pos
    for k in range(1, G):
        peer = (g + k) % G
        cp = to_grp(stats.at[g], stats.at[g], st_ss.at[k], st_rs.at[g], peer)
        cp.start()
        sends.append(cp)
    for k in range(1, G):
        peer = (g + k) % G
        to_grp(stats.at[g], stats.at[peer], st_ss.at[0], st_rs.at[peer], peer).wait_recv()
    all_top = stats[0, 0:1, :]
    for q in range(1, G):
        all_top = jnp.maximum(all_top, stats[q, 0:1, :])
    all_total = jnp.zeros((1, M), f32)
    all_pos = jnp.zeros((1, M), f32)
    for q in range(G):
        all_total = all_total + stats[q, 1:2, :] * jnp.exp(stats[q, 0:1, :] - all_top)
        all_pos = all_pos + stats[q, 2:3, :]
    log_total = all_top + jnp.log(all_total)
    loss_out[...] = log_total - all_pos
    hard_prob = jnp.where(present, jnp.exp(hard - log_total), 0.0)

    hp_hi = hard_prob.astype(bf16)
    rest = hard_prob - hp_hi.astype(f32)
    hp_mid = rest.astype(bf16)
    hp_lo = (rest - hp_mid.astype(f32)).astype(bf16)
    part_id = lax.broadcasted_iota(jnp.int32, (8, M), 0)
    hp8 = jnp.where(
        part_id == 0,
        hp_hi.astype(f32),
        jnp.where(
            part_id == 1, hp_mid.astype(f32), jnp.where(part_id == 2, hp_lo.astype(f32), 0.0)
        ),
    ).astype(bf16)

    def fill_hp(j, carry):
        hp_send[j, :, 0:cap] = dot_nt(hp8, sel[crows(j), :])
        return carry

    lax.fori_loop(0, B, fill_hp, 0)
    for k in range(1, B):
        peer = (b + k) % B
        cp = to_blk(hp_send.at[peer], hp_recv.at[b], h_ss.at[k], h_rs.at[b], peer)
        cp.start()
        sends.append(cp)
    hp_recv[b] = hp_send[b]

    def make_prob(j, carry):
        p = jnp.exp(adj[trows(j), :] - log_total) - jnp.where(hit(j), 1.0, 0.0)
        prob[trows(j), :] = p.astype(bf16)
        return carry

    lax.fori_loop(0, B, make_prob, 0)

    def fill_hard(j, carry):
        hot = sel[crows(j), :].astype(f32)
        prob[frows(j), :] = (hot * hp_hi.astype(f32)).astype(bf16)
        sel[crows(j), :] = (hot * hp_mid.astype(f32)).astype(bf16)
        return carry

    lax.fori_loop(0, B, fill_hard, 0)

    V = W if N1 <= 2048 else W // 2
    for n in range(M // V):
        cols = pl.ds(n * V, V)
        part = dot_tn(prob[:, cols], tall[...])
        part = part + dot_tn(sel[:, cols], tall[pl.ds(N1, B * cap), :])
        adj[pl.ds(n * V, V), 0:D] = part
    for k in range(1, G):
        peer = (g + k) % G
        sg_send[k - 1] = adj[trows(peer), 0:D].astype(bf16)
        cp = to_grp(sg_send.at[k - 1], sg_recv.at[k - 1], q_ss.at[k], q_rs.at[k], peer)
        cp.start()
        sends.append(cp)

    for dz in range(Z):
        j = blk_of(dz, 1 - c)
        sib_send[dz] = dot_nn(prob[trows(j), :], src[...]).astype(bf16)
        cp = to_blk(sib_send.at[dz], sib_recv.at[dz], b_ss.at[dz], b_rs.at[dz], sib)
        cp.start()
        sends.append(cp)
    for dz in list(range(1, Z)) + [0]:
        j = blk_of(dz, c)
        term = dot_nn(prob[trows(j), :], src[...])
        to_blk(sib_send.at[0], sib_recv.at[dz], b_ss.at[0], b_rs.at[dz], sib).wait_recv()
        term = term + sib_recv[dz].astype(f32)
        if dz == 0:
            tgrad[...] = term
        else:
            rs_send[dz - 1] = term.astype(bf16)
            cp = to_blk(rs_send.at[dz - 1], rs_recv.at[dz - 1], r_ss.at[dz], r_rs.at[dz], j)
            cp.start()
            sends.append(cp)

    acc = jnp.zeros((T, D), f32)
    for k in range(0, B):
        peer = (b + k) % B
        if k:
            to_blk(slots_send.at[0], slots_recv.at[peer], s_ss.at[0], s_rs.at[peer], peer).wait_recv()
            to_blk(hp_send.at[0], hp_recv.at[peer], h_ss.at[0], h_rs.at[peer], peer).wait_recv()
        hot = pool_id == want_recv[peer, 0:1, 0:cap]
        weight = jnp.sum(hp_recv[peer, :, 0:cap], axis=0, keepdims=True)
        hi = weight.astype(bf16).astype(f32)
        rows = slots_recv[peer]
        acc = acc + dot_nn(jnp.where(hot, hi, 0.0).astype(bf16), rows)
        acc = acc + dot_nn(jnp.where(hot, weight - hi, 0.0).astype(bf16), rows)
    pgrad[...] = acc

    own = adj[trows(g), 0:D]
    for k in range(1, G):
        to_grp(sg_send.at[0], sg_recv.at[k - 1], q_ss.at[0], q_rs.at[k], (g + k) % G).wait_recv()
        own = own + sg_recv[k - 1].astype(f32)
    sg_out[trows(g), :] = own.astype(bf16)
    for k in range(1, G):
        peer = (g + k) % G
        cp = to_grp(sg_out.at[trows(g)], sg_out.at[trows(g)], a_ss.at[k], a_rs.at[g], peer)
        cp.start()
        sends.append(cp)

    final = tgrad[...]
    for dz in range(1, Z):
        to_blk(rs_send.at[0], rs_recv.at[dz - 1], r_ss.at[0], r_rs.at[dz], sib).wait_recv()
        final = final + rs_recv[dz - 1].astype(f32)
    tgrad[...] = final
    for k in range(1, G):
        peer = (g + k) % G
        to_grp(sg_out.at[trows(g)], sg_out.at[trows(peer)], a_ss.at[0], a_rs.at[peer], peer).wait_recv()
    for cp in sends:
        cp.wait_send()

    @pl.when(has_up)
    def _():
        up_copy(b, 0).wait_send()

    @pl.when(has_down)
    def _():
        down_copy(b, 0).wait_send()

    def settle(step, carry):
        below = z - 1 - step
        above = z + 1 + step

        @pl.when(below >= 0)
        def _():
            block = below * 2 + c

            @pl.when(has_up)
            def _():
                up_copy(block, step + 1).wait_send()

            side_copy(block, fu_ss, step).wait_send()

        @pl.when(above < Z)
        def _():
            block = above * 2 + c

            @pl.when(has_down)
            def _():
                down_copy(block, step + 1).wait_send()

            side_copy(block, fd_ss, step).wait_send()

        return carry

    lax.fori_loop(0, Z - 1, settle, 0)


def shards(source_emb, target_emb, hard_pool, hard_index, language, margin):
    M, D = source_emb.shape
    T = target_emb.shape[0]
    B = lax.axis_size("blk")
    G = lax.axis_size("grp")
    owners = B * G
    per_block = max(2, (2 * T + owners - 1) // owners)
    cap = -(-(per_block * (M // T)) // 16) * 16
    Z = B // 2
    LP = -(-margin.shape[0] // 128) * 128
    dims = (B, G, M, T, D, cap)
    dma = pltpu.SemaphoreType.DMA
    vmem = pl.BlockSpec(memory_space=pltpu.VMEM)
    K = B * T + B * cap
    flops = 2 * M * D * (3 * B * T + 4 * B * cap)
    loss, sg, tg, pg = pl.pallas_call(
        functools.partial(kernel, dims),
        out_shape=[
            jax.ShapeDtypeStruct((1, M), f32),
            jax.ShapeDtypeStruct((M, D), bf16),
            jax.ShapeDtypeStruct((T, D), f32),
            jax.ShapeDtypeStruct((T, D), f32),
        ],
        in_specs=[vmem] * 6,
        out_specs=[vmem] * 4,
        scratch_shapes=[
            pltpu.VMEM((K, D), bf16),
            pltpu.VMEM((B * T, M), f32),
            pltpu.VMEM((K, M), bf16),
            pltpu.VMEM((B * cap, M), bf16),
            pltpu.VMEM((B, 8, 128), f32),
            pltpu.VMEM((B, 8, 128), f32),
            pltpu.VMEM((B - 1, cap, D), bf16),
            pltpu.VMEM((B, cap, D), bf16),
            pltpu.VMEM((B, cap, D), bf16),
            pltpu.VMEM((B, 8, 128), f32),
            pltpu.VMEM((B, 8, 128), f32),
            pltpu.VMEM((G, 8, M), f32),
            pltpu.VMEM((8, M), f32),
            pltpu.VMEM((8, LP), f32),
            pltpu.VMEM((G - 1, T, D), bf16),
            pltpu.VMEM((G - 1, T, D), bf16),
            pltpu.VMEM((Z, T, D), bf16),
            pltpu.VMEM((Z, T, D), bf16),
            pltpu.VMEM((Z - 1, T, D), bf16),
            pltpu.VMEM((Z - 1, T, D), bf16),
            dma((1,)), dma((B,)), dma((Z,)), dma((Z,)), dma((Z,)), dma((Z,)),
            dma((B,)), dma((B,)), dma((B,)), dma((B,)),
            dma((B,)), dma((B,)), dma((B,)), dma((B,)),
            dma((G,)), dma((G,)),
            dma((G,)), dma((G,)), dma((G,)), dma((G,)),
            dma((Z,)), dma((Z,)), dma((Z,)), dma((Z,)),
        ],
        compiler_params=pltpu.CompilerParams(
            collective_id=0, has_side_effects=True, vmem_limit_bytes=63 * 1024 * 1024
        ),
        cost_estimate=pl.CostEstimate(
            flops=flops, bytes_accessed=8 * M * D, transcendentals=2 * B * T * M
        ),
        name="loss_kernel",
    )(
        source_emb, target_emb, hard_pool, hard_index.reshape(1, M), language.reshape(1, M),
        margin.reshape(1, margin.shape[0]),
    )
    return loss.reshape(M), sg.astype(f32), tg, pg


def solution(mesh):
    in_specs = (
        P("blk", None),
        P(("grp", "blk"), None),
        P(("grp", "blk"), None),
        P("blk"),
        P("blk"),
        P(),
    )
    out_specs = (P("blk"), P("blk", None), P(("grp", "blk"), None), P(("grp", "blk"), None))
    return jax.shard_map(shards, mesh=mesh, in_specs=in_specs, out_specs=out_specs, check_vma=False)
```

```python
import functools

import jax
import jax.numpy as jnp
from jax import lax
from jax.experimental import pallas as pl
from jax.experimental.pallas import tpu as pltpu
from jax.sharding import PartitionSpec as P

neg_fill = -1e30
f32 = jnp.float32
bf16 = jnp.bfloat16
MESH = pl.DeviceIdType.MESH


def dot_nt(a, b):
    return lax.dot_general(a, b, (((1,), (1,)), ((), ())), preferred_element_type=f32)


def dot_tn(a, b):
    return lax.dot_general(a, b, (((0,), (0,)), ((), ())), preferred_element_type=f32)


def dot_nn(a, b):
    return lax.dot_general(a, b, (((1,), (0,)), ((), ())), preferred_element_type=f32)


def kernel(
    dims,
    src, tgt, pool, index_in, lang_in, margin_in,
    loss_out, sg_out, sg_scale, tgrad, pgrad,
    tall, adj, prob, sel, want_send, want_recv, picks, slots_send, slots_recv, hp_send, hp_recv,
    stats, part_stats, line, mpad, sg_send, sg_recv, sib_send, sib_recv, rs_send, rs_recv,
    t_ss, t_rs, up_ss, dn_ss, fu_ss, fd_ss, w_ss, w_rs, p_ss, p_rs, s_ss, s_rs, h_ss, h_rs, st_ss, st_rs,
    q_ss, q_rs, a_ss, a_rs, c_ss, c_rs, b_ss, b_rs, r_ss, r_rs,
):
    B, G, M, T, D, cap = dims
    Z = B // 2
    N1 = B * T
    W = 256
    b = lax.axis_index("blk")
    g = lax.axis_index("grp")
    z = b // 2
    c = b % 2
    sib = z * 2 + (1 - c)

    def blk_of(dz, core):
        return ((z + dz) % Z) * 2 + core

    def trows(j):
        return pl.ds(pl.multiple_of(j * T, T), T)

    def frows(j):
        return pl.ds(pl.multiple_of(N1 + j * cap, 16), cap)

    def crows(j):
        return pl.ds(pl.multiple_of(j * cap, 16), cap)

    def to_blk(src_ref, dst_ref, ss, rs, peer):
        return pltpu.make_async_remote_copy(
            src_ref=src_ref, dst_ref=dst_ref, send_sem=ss, recv_sem=rs,
            device_id={"blk": peer}, device_id_type=MESH,
        )

    def to_grp(src_ref, dst_ref, ss, rs, peer):
        return pltpu.make_async_remote_copy(
            src_ref=src_ref, dst_ref=dst_ref, send_sem=ss, recv_sem=rs,
            device_id={"grp": peer}, device_id_type=MESH,
        )

    def one_row(ref):
        return jnp.concatenate([ref[i : i + 1, :] for i in range(M // 128)], axis=1)

    barrier = pltpu.get_barrier_semaphore()
    for k in range(1, B):
        pl.semaphore_signal(barrier, inc=1, device_id={"blk": (b + k) % B}, device_id_type=MESH)
    for k in range(1, G):
        pl.semaphore_signal(barrier, inc=1, device_id={"grp": (g + k) % G}, device_id_type=MESH)

    pl.semaphore_wait(barrier, B - 1 + G - 1)

    sends = []
    cp = to_blk(tgt, tall.at[trows(b)], t_ss.at[0], t_rs.at[b], sib)
    cp.start()
    sends.append(cp)

    def up_copy(block, step):
        return to_blk(
            tall.at[trows(block)], tall.at[trows(block)], up_ss.at[step], t_rs.at[block], b + 2
        )

    def down_copy(block, step):
        return to_blk(
            tall.at[trows(block)], tall.at[trows(block)], dn_ss.at[step], t_rs.at[block], b - 2
        )

    def side_copy(block, sems, step):
        return to_blk(
            tall.at[trows(block)], tall.at[trows(block)], sems.at[step], t_rs.at[block], sib
        )

    has_up = z + 1 < Z
    has_down = z >= 1
    tall[trows(b), :] = tgt[...]

    @pl.when(has_up)
    def _():
        up_copy(b, 0).start()

    @pl.when(has_down)
    def _():
        down_copy(b, 0).start()


    index_row = one_row(index_in)
    owner_row = jnp.full((1, M), -1, jnp.int32)
    loc_row = jnp.zeros((1, M), jnp.int32)
    for j in range(B):
        base = (g * B + j) * T
        inside = (index_row >= base) & (index_row < base + T)
        owner_row = jnp.where(inside, j, owner_row)
        loc_row = jnp.where(inside, index_row - base, loc_row)
    present = owner_row >= 0
    col_id = lax.broadcasted_iota(jnp.int32, (T, M), 1)
    row_id = lax.broadcasted_iota(jnp.int32, (T, M), 0)

    R = max(B, 16)
    named = owner_row == lax.broadcasted_iota(jnp.int32, (R, M), 0)
    named_hot = jnp.where(named, 1.0, 0.0).astype(bf16)
    before = jnp.zeros((R, M), f32)
    for n in range(M // W):
        earlier = lax.broadcasted_iota(jnp.int32, (W, M), 0) + n * W < lax.broadcasted_iota(
            jnp.int32, (W, M), 1
        )
        step = jnp.where(earlier, 1.0, 0.0).astype(bf16)
        before = before + dot_nn(named_hot[:, n * W : (n + 1) * W], step)
    rank = jnp.sum(jnp.where(named, before, 0.0), axis=0, keepdims=True).astype(jnp.int32)
    slot = jnp.where(present, owner_row * cap + rank, -1)

    slot_id = lax.broadcasted_iota(jnp.int32, (cap, M), 0)
    loc8 = jnp.broadcast_to((loc_row + 1).astype(f32).astype(bf16), (8, M))

    def fill_sel(j, carry):
        hot = jnp.where(slot == slot_id + j * cap, 1.0, 0.0).astype(bf16)
        sel[crows(j), :] = hot
        want_send[j, :, 0:cap] = dot_nt(loc8, hot) - 1.0
        return carry

    lax.fori_loop(0, B, fill_sel, 0)

    for k in range(1, B):
        peer = (b + k) % B
        cp = to_blk(want_send.at[peer], want_recv.at[b], w_ss.at[k], w_rs.at[b], peer)
        cp.start()
        sends.append(cp)
    want_recv[b] = want_send[b]

    mpad[...] = jnp.zeros_like(mpad)
    mpad[0:1, 0 : margin_in.shape[1]] = margin_in[...]
    m_all = mpad[0:1, :]
    m_hi = m_all.astype(bf16).astype(f32)
    m_mid = (m_all - m_hi).astype(bf16).astype(f32)
    m_lo = m_all - m_hi - m_mid
    m_id = lax.broadcasted_iota(jnp.int32, mpad.shape, 0)
    m_parts = jnp.where(
        m_id == 0, m_hi, jnp.where(m_id == 1, m_mid, jnp.where(m_id == 2, m_lo, 0.0))
    ).astype(bf16)
    lang_id = lax.broadcasted_iota(jnp.int32, (mpad.shape[1], M), 0)
    lang_hot = jnp.where(one_row(lang_in) == lang_id, 1.0, 0.0).astype(bf16)
    margin_row = jnp.sum(dot_nn(m_parts, lang_hot), axis=0, keepdims=True)

    def hit(j):
        return row_id - col_id == b * M - (g * B + j) * T

    line[1:2, :] = jnp.zeros((1, M), f32)
    line[2:3, :] = margin_row

    def score(j):
        s = dot_nt(tall[trows(j), :], src[...])
        diag = hit(j)
        s = s - jnp.where(diag, line[2:3, :], 0.0)
        own_top = jnp.max(s, axis=0, keepdims=True)
        e = jnp.exp(s - own_top)
        adj[trows(j), :] = e
        part_stats[j, 0:1, :] = own_top
        part_stats[j, 1:2, :] = jnp.sum(e, axis=0, keepdims=True)
        line[1:2, :] += jnp.sum(jnp.where(diag, s, 0.0), axis=0, keepdims=True)

    score(b)

    pool_id = lax.broadcasted_iota(jnp.int32, (T, cap), 0).astype(f32)
    for k in range(0, B):
        peer = (b + k) % B
        if k:
            to_blk(want_send.at[0], want_recv.at[peer], w_ss.at[0], w_rs.at[peer], peer).wait_recv()
        hot = jnp.where(pool_id == want_recv[peer, 0:1, 0:cap], 1.0, 0.0).astype(bf16)
        picked = dot_tn(hot, pool[...]).astype(bf16)
        if k == 0:
            tall[frows(b), :] = picked
        else:
            picks[k - 1] = picked
            cp = to_blk(picks.at[k - 1], tall.at[frows(b)], p_ss.at[k], p_rs.at[b], peer)
            cp.start()
            sends.append(cp)

    def wait_t(j):
        to_blk(tgt, tall.at[trows(j)], t_ss.at[0], t_rs.at[j], sib).wait_recv()

    wait_t(sib)
    score(sib)

    def pass_on(step, carry):
        below = z - 1 - step
        above = z + 1 + step

        @pl.when(below >= 0)
        def _():
            block = below * 2 + c
            wait_t(block)

            @pl.when(has_up)
            def _():
                up_copy(block, step + 1).start()

            side_copy(block, fu_ss, step).start()

        @pl.when(above < Z)
        def _():
            block = above * 2 + c
            wait_t(block)

            @pl.when(has_down)
            def _():
                down_copy(block, step + 1).start()

            side_copy(block, fd_ss, step).start()

        def use(q, inner):
            at = jnp.where(q % 2 == 0, below, above)

            @pl.when((at >= 0) & (at < Z))
            def _():
                far = q // 2
                block = at * 2 + (c + far) % 2

                @pl.when(far == 1)
                def _():
                    wait_t(block)

                score(block)

            return inner

        lax.fori_loop(0, 4, use, 0)
        return carry

    def fill_slots(j, carry):
        slots_send[j] = dot_nn(sel[crows(j), :], src[...]).astype(bf16)
        return carry

    lax.fori_loop(0, B, fill_slots, 0)
    lax.fori_loop(0, Z - 1, pass_on, 0)
    for k in range(1, B):
        peer = (b + k) % B
        cp = to_blk(slots_send.at[peer], slots_recv.at[b], s_ss.at[k], s_rs.at[b], peer)
        cp.start()
        sends.append(cp)
    slots_recv[b] = slots_send[b]
    pos = line[1:2, :]
    for k in range(1, B):
        peer = (b + k) % B
        to_blk(picks.at[0], tall.at[frows(peer)], p_ss.at[0], p_rs.at[peer], peer).wait_recv()

    def hard_part(j, acc):
        s = dot_nt(tall[frows(j), :], src[...])
        return acc + jnp.sum(s * sel[crows(j), :].astype(f32), axis=0, keepdims=True)

    hard = lax.fori_loop(0, B, hard_part, jnp.zeros((1, M), f32))
    hard = jnp.where(present, hard, neg_fill)
    top = hard
    for j in range(B):
        top = jnp.maximum(top, part_stats[j, 0:1, :])

    total = jnp.where(present, jnp.exp(hard - top), 0.0)
    for j in range(B):
        total = total + part_stats[j, 1:2, :] * jnp.exp(part_stats[j, 0:1, :] - top)
    stats[g, 0:1, :] = top
    stats[g, 1:2, :] = total
    stats[g, 2:3, :] = pos
    for k in range(1, G):
        peer = (g + k) % G
        cp = to_grp(stats.at[g], stats.at[g], st_ss.at[k], st_rs.at[g], peer)
        cp.start()
        sends.append(cp)
    for k in range(1, G):
        peer = (g + k) % G
        to_grp(stats.at[g], stats.at[peer], st_ss.at[0], st_rs.at[peer], peer).wait_recv()
    all_top = stats[0, 0:1, :]
    for q in range(1, G):
        all_top = jnp.maximum(all_top, stats[q, 0:1, :])
    all_total = jnp.zeros((1, M), f32)
    all_pos = jnp.zeros((1, M), f32)
    for q in range(G):
        all_total = all_total + stats[q, 1:2, :] * jnp.exp(stats[q, 0:1, :] - all_top)
        all_pos = all_pos + stats[q, 2:3, :]
    log_total = all_top + jnp.log(all_total)
    loss = log_total - all_pos
    for i in range(M // 128):
        loss_out[i : i + 1, :] = loss[:, i * 128 : (i + 1) * 128]
    hard_prob = jnp.where(present, jnp.exp(hard - log_total), 0.0)

    def make_prob(j, carry):
        scale = jnp.exp(part_stats[j, 0:1, :] - log_total)
        p = adj[trows(j), :] * scale - jnp.where(hit(j), 1.0, 0.0)
        prob[trows(j), :] = p.astype(bf16)
        return carry

    lax.fori_loop(0, B, make_prob, 0)

    for dz in range(Z):
        j = blk_of(dz, 1 - c)
        sib_send[dz] = dot_nn(prob[trows(j), :], src[...]).astype(bf16)
        cp = to_blk(sib_send.at[dz], sib_recv.at[dz], b_ss.at[dz], b_rs.at[dz], sib)
        cp.start()
        sends.append(cp)
    for dz in list(range(1, Z)) + [0]:
        j = blk_of(dz, c)
        term = dot_nn(prob[trows(j), :], src[...])
        to_blk(sib_send.at[0], sib_recv.at[dz], b_ss.at[0], b_rs.at[dz], sib).wait_recv()
        term = term + sib_recv[dz].astype(f32)
        if dz == 0:
            tgrad[...] = term
        else:
            rs_send[dz - 1] = term.astype(bf16)
            cp = to_blk(rs_send.at[dz - 1], rs_recv.at[dz - 1], r_ss.at[dz], r_rs.at[dz], j)
            cp.start()
            sends.append(cp)

    hp_hi = hard_prob.astype(bf16)
    rest = hard_prob - hp_hi.astype(f32)
    hp_mid = rest.astype(bf16)
    hp_lo = (rest - hp_mid.astype(f32)).astype(bf16)
    part_id = lax.broadcasted_iota(jnp.int32, (8, M), 0)
    hp8 = jnp.where(
        part_id == 0,
        hp_hi.astype(f32),
        jnp.where(
            part_id == 1, hp_mid.astype(f32), jnp.where(part_id == 2, hp_lo.astype(f32), 0.0)
        ),
    ).astype(bf16)

    def fill_hp(j, carry):
        hp_send[j, :, 0:cap] = dot_nt(hp8, sel[crows(j), :])
        return carry

    lax.fori_loop(0, B, fill_hp, 0)
    for k in range(1, B):
        peer = (b + k) % B
        cp = to_blk(hp_send.at[peer], hp_recv.at[b], h_ss.at[k], h_rs.at[b], peer)
        cp.start()
        sends.append(cp)
    hp_recv[b] = hp_send[b]

    def fill_hard(j, carry):
        hot = sel[crows(j), :].astype(f32)
        prob[frows(j), :] = (hot * hp_hi.astype(f32)).astype(bf16)
        sel[crows(j), :] = (hot * hp_mid.astype(f32)).astype(bf16)
        return carry

    lax.fori_loop(0, B, fill_hard, 0)

    V = W if N1 <= 2048 else W // 2
    for n in range(M // V):
        cols = pl.ds(n * V, V)
        part = dot_tn(prob[:, cols], tall[...])
        part = part + dot_tn(sel[:, cols], tall[pl.ds(N1, B * cap), :])
        adj[pl.ds(n * V, V), 0:D] = part
    for k in range(1, G):
        peer = (g + k) % G
        sg_send[k - 1] = adj[trows(peer), 0:D].astype(bf16)
        cp = to_grp(sg_send.at[k - 1], sg_recv.at[k - 1], q_ss.at[k], q_rs.at[k], peer)
        cp.start()
        sends.append(cp)

    acc = jnp.zeros((T, D), f32)
    for k in range(0, B):
        peer = (b + k) % B
        if k:
            to_blk(slots_send.at[0], slots_recv.at[peer], s_ss.at[0], s_rs.at[peer], peer).wait_recv()
            to_blk(hp_send.at[0], hp_recv.at[peer], h_ss.at[0], h_rs.at[peer], peer).wait_recv()
        hot = pool_id == want_recv[peer, 0:1, 0:cap]
        weight = jnp.sum(hp_recv[peer, :, 0:cap], axis=0, keepdims=True)
        hi = weight.astype(bf16).astype(f32)
        rows = slots_recv[peer]
        acc = acc + dot_nn(jnp.where(hot, hi, 0.0).astype(bf16), rows)
        acc = acc + dot_nn(jnp.where(hot, weight - hi, 0.0).astype(bf16), rows)
    pgrad[...] = acc

    own = adj[trows(g), 0:D]
    for k in range(1, G):
        to_grp(sg_send.at[0], sg_recv.at[k - 1], q_ss.at[0], q_rs.at[k], (g + k) % G).wait_recv()
        own = own + sg_recv[k - 1].astype(f32)
    limit = jnp.maximum(jnp.max(jnp.abs(own), axis=0, keepdims=True), 1e-30)
    coded = jnp.floor(own * (32767.0 / limit) + 0.5)
    sg_out[trows(g), :] = coded.astype(jnp.int32).astype(jnp.int16)
    sg_scale[g] = jnp.broadcast_to(limit * (1.0 / 32767.0), (8, D))
    for k in range(1, G):
        peer = (g + k) % G
        cp = to_grp(sg_out.at[trows(g)], sg_out.at[trows(g)], a_ss.at[k], a_rs.at[g], peer)
        cp.start()
        sends.append(cp)
        cp = to_grp(sg_scale.at[g], sg_scale.at[g], c_ss.at[k], c_rs.at[g], peer)
        cp.start()
        sends.append(cp)

    final = tgrad[...]
    for dz in range(1, Z):
        to_blk(rs_send.at[0], rs_recv.at[dz - 1], r_ss.at[0], r_rs.at[dz], sib).wait_recv()
        final = final + rs_recv[dz - 1].astype(f32)
    tgrad[...] = final
    for k in range(1, G):
        peer = (g + k) % G
        to_grp(sg_out.at[trows(g)], sg_out.at[trows(peer)], a_ss.at[0], a_rs.at[peer], peer).wait_recv()
        to_grp(sg_scale.at[g], sg_scale.at[peer], c_ss.at[0], c_rs.at[peer], peer).wait_recv()
    for cp in sends:
        cp.wait_send()

    @pl.when(has_up)
    def _():
        up_copy(b, 0).wait_send()

    @pl.when(has_down)
    def _():
        down_copy(b, 0).wait_send()

    def settle(step, carry):
        below = z - 1 - step
        above = z + 1 + step

        @pl.when(below >= 0)
        def _():
            block = below * 2 + c

            @pl.when(has_up)
            def _():
                up_copy(block, step + 1).wait_send()

            side_copy(block, fu_ss, step).wait_send()

        @pl.when(above < Z)
        def _():
            block = above * 2 + c

            @pl.when(has_down)
            def _():
                down_copy(block, step + 1).wait_send()

            side_copy(block, fd_ss, step).wait_send()

        return carry

    lax.fori_loop(0, Z - 1, settle, 0)


def shards(source_emb, target_emb, hard_pool, hard_index, language, margin):
    M, D = source_emb.shape
    T = target_emb.shape[0]
    B = lax.axis_size("blk")
    G = lax.axis_size("grp")
    owners = B * G
    per_block = max(2, (2 * T + owners - 1) // owners)
    cap = -(-(per_block * (M // T)) // 16) * 16
    Z = B // 2
    LP = -(-margin.shape[0] // 128) * 128
    dims = (B, G, M, T, D, cap)
    dma = pltpu.SemaphoreType.DMA
    vmem = pl.BlockSpec(memory_space=pltpu.VMEM)
    K = B * T + B * cap
    flops = 2 * M * D * (3 * B * T + 4 * B * cap)
    loss, coded, scale, tg, pg = pl.pallas_call(
        functools.partial(kernel, dims),
        out_shape=[
            jax.ShapeDtypeStruct((M // 128, 128), f32),
            jax.ShapeDtypeStruct((M, D), jnp.int16),
            jax.ShapeDtypeStruct((G, 8, D), f32),
            jax.ShapeDtypeStruct((T, D), f32),
            jax.ShapeDtypeStruct((T, D), f32),
        ],
        in_specs=[vmem] * 6,
        out_specs=[vmem] * 5,
        scratch_shapes=[
            pltpu.VMEM((K, D), bf16),
            pltpu.VMEM((B * T, M), f32),
            pltpu.VMEM((K, M), bf16),
            pltpu.VMEM((B * cap, M), bf16),
            pltpu.VMEM((B, 8, 128), f32),
            pltpu.VMEM((B, 8, 128), f32),
            pltpu.VMEM((B - 1, cap, D), bf16),
            pltpu.VMEM((B, cap, D), bf16),
            pltpu.VMEM((B, cap, D), bf16),
            pltpu.VMEM((B, 8, 128), f32),
            pltpu.VMEM((B, 8, 128), f32),
            pltpu.VMEM((G, 8, M), f32),
            pltpu.VMEM((B, 8, M), f32),
            pltpu.VMEM((8, M), f32),
            pltpu.VMEM((8, LP), f32),
            pltpu.VMEM((G - 1, T, D), bf16),
            pltpu.VMEM((G - 1, T, D), bf16),
            pltpu.VMEM((Z, T, D), bf16),
            pltpu.VMEM((Z, T, D), bf16),
            pltpu.VMEM((Z - 1, T, D), bf16),
            pltpu.VMEM((Z - 1, T, D), bf16),
            dma((1,)), dma((B,)), dma((Z,)), dma((Z,)), dma((Z,)), dma((Z,)),
            dma((B,)), dma((B,)), dma((B,)), dma((B,)),
            dma((B,)), dma((B,)), dma((B,)), dma((B,)),
            dma((G,)), dma((G,)),
            dma((G,)), dma((G,)), dma((G,)), dma((G,)), dma((G,)), dma((G,)),
            dma((Z,)), dma((Z,)), dma((Z,)), dma((Z,)),
        ],
        compiler_params=pltpu.CompilerParams(
            collective_id=0, has_side_effects=True, vmem_limit_bytes=63 * 1024 * 1024
        ),
        cost_estimate=pl.CostEstimate(
            flops=flops, bytes_accessed=8 * M * D, transcendentals=2 * B * T * M
        ),
        name="loss_kernel",
    )(
        source_emb, target_emb, hard_pool, hard_index.reshape(M // 128, 128), language.reshape(M // 128, 128),
        margin.reshape(1, margin.shape[0]),
    )
    sg = (coded.reshape(G, T, D).astype(f32) * scale[:, 0:1, :]).reshape(M, D)
    return loss.reshape(M), sg, tg, pg


def solution(mesh):
    in_specs = (
        P("blk", None),
        P(("grp", "blk"), None),
        P(("grp", "blk"), None),
        P("blk"),
        P("blk"),
        P(),
    )
    out_specs = (P("blk"), P("blk", None), P(("grp", "blk"), None), P(("grp", "blk"), None))
    return jax.shard_map(shards, mesh=mesh, in_specs=in_specs, out_specs=out_specs, check_vma=False)
```

```python
import functools

import jax
import jax.numpy as jnp
from jax import lax
from jax.experimental import pallas as pl
from jax.experimental.pallas import tpu as pltpu
from jax.sharding import PartitionSpec as P

neg_fill = -1e30
f32 = jnp.float32
bf16 = jnp.bfloat16
MESH = pl.DeviceIdType.MESH


def dot_nt(a, b):
    return lax.dot_general(a, b, (((1,), (1,)), ((), ())), preferred_element_type=f32)


def dot_tn(a, b):
    return lax.dot_general(a, b, (((0,), (0,)), ((), ())), preferred_element_type=f32)


def dot_nn(a, b):
    return lax.dot_general(a, b, (((1,), (0,)), ((), ())), preferred_element_type=f32)


def kernel(
    dims,
    src, tgt, pool, index_in, lang_in, margin_in,
    loss_out, sg_out, sg_scale, tgrad, pgrad,
    tall, adj, prob, sel, want_send, want_recv, picks, slots_send, slots_recv, hp_send, hp_recv,
    stats, part_stats, line, mpad, sg_send, sg_recv, sib_send, sib_recv, rs_send, rs_recv,
    t_ss, t_rs, up_ss, dn_ss, fu_ss, fd_ss, w_ss, w_rs, p_ss, p_rs, s_ss, s_rs, h_ss, h_rs, st_ss, st_rs,
    q_ss, q_rs, a_ss, a_rs, c_ss, c_rs, b_ss, b_rs, r_ss, r_rs,
):
    B, G, M, T, D, cap = dims
    Z = B // 2
    N1 = B * T
    W = 256
    b = lax.axis_index("blk")
    g = lax.axis_index("grp")
    z = b // 2
    c = b % 2
    sib = z * 2 + (1 - c)

    def blk_of(dz, core):
        return ((z + dz) % Z) * 2 + core

    def trows(j):
        return pl.ds(pl.multiple_of(j * T, T), T)

    def frows(j):
        return pl.ds(pl.multiple_of(N1 + j * cap, 16), cap)

    def crows(j):
        return pl.ds(pl.multiple_of(j * cap, 16), cap)

    def to_blk(src_ref, dst_ref, ss, rs, peer):
        return pltpu.make_async_remote_copy(
            src_ref=src_ref, dst_ref=dst_ref, send_sem=ss, recv_sem=rs,
            device_id={"blk": peer}, device_id_type=MESH,
        )

    def to_grp(src_ref, dst_ref, ss, rs, peer):
        return pltpu.make_async_remote_copy(
            src_ref=src_ref, dst_ref=dst_ref, send_sem=ss, recv_sem=rs,
            device_id={"grp": peer}, device_id_type=MESH,
        )

    def one_row(ref):
        return jnp.concatenate([ref[i : i + 1, :] for i in range(M // 128)], axis=1)

    barrier = pltpu.get_barrier_semaphore()
    for k in range(1, B):
        pl.semaphore_signal(barrier, inc=1, device_id={"blk": (b + k) % B}, device_id_type=MESH)
    for k in range(1, G):
        pl.semaphore_signal(barrier, inc=1, device_id={"grp": (g + k) % G}, device_id_type=MESH)

    pl.semaphore_wait(barrier, B - 1 + G - 1)

    sends = []
    cp = to_blk(tgt, tall.at[trows(b)], t_ss.at[0], t_rs.at[b], sib)
    cp.start()
    sends.append(cp)

    def up_copy(block, step):
        return to_blk(
            tall.at[trows(block)], tall.at[trows(block)], up_ss.at[step], t_rs.at[block], b + 2
        )

    def down_copy(block, step):
        return to_blk(
            tall.at[trows(block)], tall.at[trows(block)], dn_ss.at[step], t_rs.at[block], b - 2
        )

    def side_copy(block, sems, step):
        return to_blk(
            tall.at[trows(block)], tall.at[trows(block)], sems.at[step], t_rs.at[block], sib
        )

    has_up = z + 1 < Z
    has_down = z >= 1
    tall[trows(b), :] = tgt[...]

    @pl.when(has_up)
    def _():
        up_copy(b, 0).start()

    @pl.when(has_down)
    def _():
        down_copy(b, 0).start()


    index_row = one_row(index_in)
    owner_row = jnp.full((1, M), -1, jnp.int32)
    loc_row = jnp.zeros((1, M), jnp.int32)
    for j in range(B):
        base = (g * B + j) * T
        inside = (index_row >= base) & (index_row < base + T)
        owner_row = jnp.where(inside, j, owner_row)
        loc_row = jnp.where(inside, index_row - base, loc_row)
    present = owner_row >= 0
    col_id = lax.broadcasted_iota(jnp.int32, (T, M), 1)
    row_id = lax.broadcasted_iota(jnp.int32, (T, M), 0)

    R = max(B, 16)
    named = owner_row == lax.broadcasted_iota(jnp.int32, (R, M), 0)
    named_hot = jnp.where(named, 1.0, 0.0).astype(bf16)
    before = jnp.zeros((R, M), f32)
    for n in range(M // W):
        earlier = lax.broadcasted_iota(jnp.int32, (W, M), 0) + n * W < lax.broadcasted_iota(
            jnp.int32, (W, M), 1
        )
        step = jnp.where(earlier, 1.0, 0.0).astype(bf16)
        before = before + dot_nn(named_hot[:, n * W : (n + 1) * W], step)
    rank = jnp.sum(jnp.where(named, before, 0.0), axis=0, keepdims=True).astype(jnp.int32)
    slot = jnp.where(present, owner_row * cap + rank, -1)

    slot_id = lax.broadcasted_iota(jnp.int32, (cap, M), 0)
    loc8 = jnp.broadcast_to((loc_row + 1).astype(f32).astype(bf16), (8, M))

    def fill_sel(j, carry):
        hot = jnp.where(slot == slot_id + j * cap, 1.0, 0.0).astype(bf16)
        sel[crows(j), :] = hot
        want_send[j, :, 0:cap] = dot_nt(loc8, hot) - 1.0
        return carry

    lax.fori_loop(0, B, fill_sel, 0)

    for k in range(1, B):
        peer = (b + k) % B
        cp = to_blk(want_send.at[peer], want_recv.at[b], w_ss.at[k], w_rs.at[b], peer)
        cp.start()
        sends.append(cp)
    want_recv[b] = want_send[b]

    mpad[...] = jnp.zeros_like(mpad)
    mpad[0:1, 0 : margin_in.shape[1]] = margin_in[...]
    m_all = mpad[0:1, :]
    m_hi = m_all.astype(bf16).astype(f32)
    m_mid = (m_all - m_hi).astype(bf16).astype(f32)
    m_lo = m_all - m_hi - m_mid
    m_id = lax.broadcasted_iota(jnp.int32, mpad.shape, 0)
    m_parts = jnp.where(
        m_id == 0, m_hi, jnp.where(m_id == 1, m_mid, jnp.where(m_id == 2, m_lo, 0.0))
    ).astype(bf16)
    lang_id = lax.broadcasted_iota(jnp.int32, (mpad.shape[1], M), 0)
    lang_hot = jnp.where(one_row(lang_in) == lang_id, 1.0, 0.0).astype(bf16)
    margin_row = jnp.sum(dot_nn(m_parts, lang_hot), axis=0, keepdims=True)

    def hit(j):
        return row_id - col_id == b * M - (g * B + j) * T

    line[1:2, :] = jnp.zeros((1, M), f32)
    line[2:3, :] = margin_row

    def score(j):
        s = dot_nt(tall[trows(j), :], src[...])
        diag = hit(j)
        s = s - jnp.where(diag, line[2:3, :], 0.0)
        own_top = jnp.max(s, axis=0, keepdims=True)
        e = jnp.exp(s - own_top)
        adj[trows(j), :] = e
        part_stats[j, 0:1, :] = own_top
        part_stats[j, 1:2, :] = jnp.sum(e, axis=0, keepdims=True)
        line[1:2, :] += jnp.sum(jnp.where(diag, s, 0.0), axis=0, keepdims=True)

    score(b)

    pool_id = lax.broadcasted_iota(jnp.int32, (T, cap), 0).astype(f32)
    for k in range(0, B):
        peer = (b + k) % B
        if k:
            to_blk(want_send.at[0], want_recv.at[peer], w_ss.at[0], w_rs.at[peer], peer).wait_recv()
        hot = jnp.where(pool_id == want_recv[peer, 0:1, 0:cap], 1.0, 0.0).astype(bf16)
        picked = dot_tn(hot, pool[...]).astype(bf16)
        if k == 0:
            tall[frows(b), :] = picked
        else:
            picks[k - 1] = picked
            cp = to_blk(picks.at[k - 1], tall.at[frows(b)], p_ss.at[k], p_rs.at[b], peer)
            cp.start()
            sends.append(cp)

    def wait_t(j):
        to_blk(tgt, tall.at[trows(j)], t_ss.at[0], t_rs.at[j], sib).wait_recv()

    wait_t(sib)
    score(sib)

    def pass_on(step, carry):
        below = z - 1 - step
        above = z + 1 + step

        @pl.when(below >= 0)
        def _():
            block = below * 2 + c
            wait_t(block)

            @pl.when(has_up)
            def _():
                up_copy(block, step + 1).start()

            side_copy(block, fu_ss, step).start()

        @pl.when(above < Z)
        def _():
            block = above * 2 + c
            wait_t(block)

            @pl.when(has_down)
            def _():
                down_copy(block, step + 1).start()

            side_copy(block, fd_ss, step).start()

        def use(q, inner):
            at = jnp.where(q % 2 == 0, below, above)

            @pl.when((at >= 0) & (at < Z))
            def _():
                far = q // 2
                block = at * 2 + (c + far) % 2

                @pl.when(far == 1)
                def _():
                    wait_t(block)

                score(block)

            return inner

        lax.fori_loop(0, 4, use, 0)
        return carry

    def fill_slots(j, carry):
        slots_send[j] = dot_nn(sel[crows(j), :], src[...]).astype(bf16)
        return carry

    lax.fori_loop(0, B, fill_slots, 0)
    lax.fori_loop(0, Z - 1, pass_on, 0)
    pos = line[1:2, :]
    for k in range(1, B):
        peer = (b + k) % B
        to_blk(picks.at[0], tall.at[frows(peer)], p_ss.at[0], p_rs.at[peer], peer).wait_recv()

    def hard_part(j, acc):
        s = dot_nt(tall[frows(j), :], src[...])
        return acc + jnp.sum(s * sel[crows(j), :].astype(f32), axis=0, keepdims=True)

    hard = lax.fori_loop(0, B, hard_part, jnp.zeros((1, M), f32))
    hard = jnp.where(present, hard, neg_fill)
    top = hard
    for j in range(B):
        top = jnp.maximum(top, part_stats[j, 0:1, :])

    total = jnp.where(present, jnp.exp(hard - top), 0.0)
    for j in range(B):
        total = total + part_stats[j, 1:2, :] * jnp.exp(part_stats[j, 0:1, :] - top)
    stats[g, 0:1, :] = top
    stats[g, 1:2, :] = total
    stats[g, 2:3, :] = pos
    for k in range(1, G):
        peer = (g + k) % G
        cp = to_grp(stats.at[g], stats.at[g], st_ss.at[k], st_rs.at[g], peer)
        cp.start()
        sends.append(cp)
    for k in range(1, B):
        peer = (b + k) % B
        cp = to_blk(slots_send.at[peer], slots_recv.at[b], s_ss.at[k], s_rs.at[b], peer)
        cp.start()
        sends.append(cp)
    slots_recv[b] = slots_send[b]
    for k in range(1, G):
        peer = (g + k) % G
        to_grp(stats.at[g], stats.at[peer], st_ss.at[0], st_rs.at[peer], peer).wait_recv()
    all_top = stats[0, 0:1, :]
    for q in range(1, G):
        all_top = jnp.maximum(all_top, stats[q, 0:1, :])
    all_total = jnp.zeros((1, M), f32)
    all_pos = jnp.zeros((1, M), f32)
    for q in range(G):
        all_total = all_total + stats[q, 1:2, :] * jnp.exp(stats[q, 0:1, :] - all_top)
        all_pos = all_pos + stats[q, 2:3, :]
    log_total = all_top + jnp.log(all_total)
    loss = log_total - all_pos
    for i in range(M // 128):
        loss_out[i : i + 1, :] = loss[:, i * 128 : (i + 1) * 128]
    hard_prob = jnp.where(present, jnp.exp(hard - log_total), 0.0)

    hp_hi = hard_prob.astype(bf16)
    rest = hard_prob - hp_hi.astype(f32)
    hp_mid = rest.astype(bf16)
    hp_lo = (rest - hp_mid.astype(f32)).astype(bf16)
    part_id = lax.broadcasted_iota(jnp.int32, (8, M), 0)
    hp8 = jnp.where(
        part_id == 0,
        hp_hi.astype(f32),
        jnp.where(
            part_id == 1, hp_mid.astype(f32), jnp.where(part_id == 2, hp_lo.astype(f32), 0.0)
        ),
    ).astype(bf16)

    def fill_hp(j, carry):
        hp_send[j, :, 0:cap] = dot_nt(hp8, sel[crows(j), :])
        return carry

    lax.fori_loop(0, B, fill_hp, 0)
    for k in range(1, B):
        peer = (b + k) % B
        cp = to_blk(hp_send.at[peer], hp_recv.at[b], h_ss.at[k], h_rs.at[b], peer)
        cp.start()
        sends.append(cp)
    hp_recv[b] = hp_send[b]

    def make_prob(j, carry):
        scale = jnp.exp(part_stats[j, 0:1, :] - log_total)
        p = adj[trows(j), :] * scale - jnp.where(hit(j), 1.0, 0.0)
        prob[trows(j), :] = p.astype(bf16)
        return carry

    lax.fori_loop(0, B, make_prob, 0)

    def fill_hard(j, carry):
        hot = sel[crows(j), :].astype(f32)
        prob[frows(j), :] = (hot * hp_hi.astype(f32)).astype(bf16)
        sel[crows(j), :] = (hot * hp_mid.astype(f32)).astype(bf16)
        return carry

    lax.fori_loop(0, B, fill_hard, 0)

    V = W if N1 <= 2048 else W // 2
    for n in range(M // V):
        cols = pl.ds(n * V, V)
        part = dot_tn(prob[:, cols], tall[...])
        part = part + dot_tn(sel[:, cols], tall[pl.ds(N1, B * cap), :])
        adj[pl.ds(n * V, V), 0:D] = part
    for k in range(1, G):
        peer = (g + k) % G
        sg_send[k - 1] = adj[trows(peer), 0:D].astype(bf16)
        cp = to_grp(sg_send.at[k - 1], sg_recv.at[k - 1], q_ss.at[k], q_rs.at[k], peer)
        cp.start()
        sends.append(cp)

    for dz in range(Z):
        j = blk_of(dz, 1 - c)
        sib_send[dz] = dot_nn(prob[trows(j), :], src[...]).astype(bf16)
        cp = to_blk(sib_send.at[dz], sib_recv.at[dz], b_ss.at[dz], b_rs.at[dz], sib)
        cp.start()
        sends.append(cp)
    for dz in list(range(1, Z)) + [0]:
        j = blk_of(dz, c)
        term = dot_nn(prob[trows(j), :], src[...])
        to_blk(sib_send.at[0], sib_recv.at[dz], b_ss.at[0], b_rs.at[dz], sib).wait_recv()
        term = term + sib_recv[dz].astype(f32)
        if dz == 0:
            tgrad[...] = term
        else:
            rs_send[dz - 1] = term.astype(bf16)
            cp = to_blk(rs_send.at[dz - 1], rs_recv.at[dz - 1], r_ss.at[dz], r_rs.at[dz], j)
            cp.start()
            sends.append(cp)

    own = adj[trows(g), 0:D]
    for k in range(1, G):
        to_grp(sg_send.at[0], sg_recv.at[k - 1], q_ss.at[0], q_rs.at[k], (g + k) % G).wait_recv()
        own = own + sg_recv[k - 1].astype(f32)
    limit = jnp.maximum(jnp.max(jnp.abs(own), axis=0, keepdims=True), 1e-30)
    coded = jnp.floor(own * (32767.0 / limit) + 0.5)
    sg_out[trows(g), :] = coded.astype(jnp.int32).astype(jnp.int16)
    sg_scale[g] = jnp.broadcast_to(limit * (1.0 / 32767.0), (8, D))
    for k in range(1, G):
        peer = (g + k) % G
        cp = to_grp(sg_out.at[trows(g)], sg_out.at[trows(g)], a_ss.at[k], a_rs.at[g], peer)
        cp.start()
        sends.append(cp)
        cp = to_grp(sg_scale.at[g], sg_scale.at[g], c_ss.at[k], c_rs.at[g], peer)
        cp.start()
        sends.append(cp)

    acc = jnp.zeros((T, D), f32)
    for k in range(0, B):
        peer = (b + k) % B
        if k:
            to_blk(slots_send.at[0], slots_recv.at[peer], s_ss.at[0], s_rs.at[peer], peer).wait_recv()
            to_blk(hp_send.at[0], hp_recv.at[peer], h_ss.at[0], h_rs.at[peer], peer).wait_recv()
        hot = pool_id == want_recv[peer, 0:1, 0:cap]
        weight = jnp.sum(hp_recv[peer, :, 0:cap], axis=0, keepdims=True)
        hi = weight.astype(bf16).astype(f32)
        rows = slots_recv[peer]
        acc = acc + dot_nn(jnp.where(hot, hi, 0.0).astype(bf16), rows)
        acc = acc + dot_nn(jnp.where(hot, weight - hi, 0.0).astype(bf16), rows)
    pgrad[...] = acc

    final = tgrad[...]
    for dz in range(1, Z):
        to_blk(rs_send.at[0], rs_recv.at[dz - 1], r_ss.at[0], r_rs.at[dz], sib).wait_recv()
        final = final + rs_recv[dz - 1].astype(f32)
    tgrad[...] = final
    for k in range(1, G):
        peer = (g + k) % G
        to_grp(sg_out.at[trows(g)], sg_out.at[trows(peer)], a_ss.at[0], a_rs.at[peer], peer).wait_recv()
        to_grp(sg_scale.at[g], sg_scale.at[peer], c_ss.at[0], c_rs.at[peer], peer).wait_recv()
    for cp in sends:
        cp.wait_send()

    @pl.when(has_up)
    def _():
        up_copy(b, 0).wait_send()

    @pl.when(has_down)
    def _():
        down_copy(b, 0).wait_send()

    def settle(step, carry):
        below = z - 1 - step
        above = z + 1 + step

        @pl.when(below >= 0)
        def _():
            block = below * 2 + c

            @pl.when(has_up)
            def _():
                up_copy(block, step + 1).wait_send()

            side_copy(block, fu_ss, step).wait_send()

        @pl.when(above < Z)
        def _():
            block = above * 2 + c

            @pl.when(has_down)
            def _():
                down_copy(block, step + 1).wait_send()

            side_copy(block, fd_ss, step).wait_send()

        return carry

    lax.fori_loop(0, Z - 1, settle, 0)


def shards(source_emb, target_emb, hard_pool, hard_index, language, margin):
    M, D = source_emb.shape
    T = target_emb.shape[0]
    B = lax.axis_size("blk")
    G = lax.axis_size("grp")
    owners = B * G
    per_block = max(2, (2 * T + owners - 1) // owners)
    cap = -(-(per_block * (M // T)) // 16) * 16
    Z = B // 2
    LP = -(-margin.shape[0] // 128) * 128
    dims = (B, G, M, T, D, cap)
    dma = pltpu.SemaphoreType.DMA
    vmem = pl.BlockSpec(memory_space=pltpu.VMEM)
    K = B * T + B * cap
    flops = 2 * M * D * (3 * B * T + 4 * B * cap)
    loss, coded, scale, tg, pg = pl.pallas_call(
        functools.partial(kernel, dims),
        out_shape=[
            jax.ShapeDtypeStruct((M // 128, 128), f32),
            jax.ShapeDtypeStruct((M, D), jnp.int16),
            jax.ShapeDtypeStruct((G, 8, D), f32),
            jax.ShapeDtypeStruct((T, D), f32),
            jax.ShapeDtypeStruct((T, D), f32),
        ],
        in_specs=[vmem] * 6,
        out_specs=[vmem] * 5,
        scratch_shapes=[
            pltpu.VMEM((K, D), bf16),
            pltpu.VMEM((B * T, M), f32),
            pltpu.VMEM((K, M), bf16),
            pltpu.VMEM((B * cap, M), bf16),
            pltpu.VMEM((B, 8, 128), f32),
            pltpu.VMEM((B, 8, 128), f32),
            pltpu.VMEM((B - 1, cap, D), bf16),
            pltpu.VMEM((B, cap, D), bf16),
            pltpu.VMEM((B, cap, D), bf16),
            pltpu.VMEM((B, 8, 128), f32),
            pltpu.VMEM((B, 8, 128), f32),
            pltpu.VMEM((G, 8, M), f32),
            pltpu.VMEM((B, 8, M), f32),
            pltpu.VMEM((8, M), f32),
            pltpu.VMEM((8, LP), f32),
            pltpu.VMEM((G - 1, T, D), bf16),
            pltpu.VMEM((G - 1, T, D), bf16),
            pltpu.VMEM((Z, T, D), bf16),
            pltpu.VMEM((Z, T, D), bf16),
            pltpu.VMEM((Z - 1, T, D), bf16),
            pltpu.VMEM((Z - 1, T, D), bf16),
            dma((1,)), dma((B,)), dma((Z,)), dma((Z,)), dma((Z,)), dma((Z,)),
            dma((B,)), dma((B,)), dma((B,)), dma((B,)),
            dma((B,)), dma((B,)), dma((B,)), dma((B,)),
            dma((G,)), dma((G,)),
            dma((G,)), dma((G,)), dma((G,)), dma((G,)), dma((G,)), dma((G,)),
            dma((Z,)), dma((Z,)), dma((Z,)), dma((Z,)),
        ],
        compiler_params=pltpu.CompilerParams(
            collective_id=0, has_side_effects=True, vmem_limit_bytes=63 * 1024 * 1024
        ),
        cost_estimate=pl.CostEstimate(
            flops=flops, bytes_accessed=8 * M * D, transcendentals=2 * B * T * M
        ),
        name="loss_kernel",
    )(
        source_emb, target_emb, hard_pool, hard_index.reshape(M // 128, 128), language.reshape(M // 128, 128),
        margin.reshape(1, margin.shape[0]),
    )
    sg = (coded.reshape(G, T, D).astype(f32) * scale[:, 0:1, :]).reshape(M, D)
    return loss.reshape(M), sg, tg, pg


def solution(mesh):
    in_specs = (
        P("blk", None),
        P(("grp", "blk"), None),
        P(("grp", "blk"), None),
        P("blk"),
        P("blk"),
        P(),
    )
    out_specs = (P("blk"), P("blk", None), P(("grp", "blk"), None), P(("grp", "blk"), None))
    return jax.shard_map(shards, mesh=mesh, in_specs=in_specs, out_specs=out_specs, check_vma=False)
```
